128 devices in a mesh: group: 4 (over z_lo, core), blk: 32 (over y, x, z_hi).
Axes of the slice: x: 4, y: 4, z: 4 (z_hi: 2, z_lo: 2; z = z_hi * 2 + z_lo), core: 2. Of those that a mesh axis runs over, the one named last changes fastest.
Arguments:
- query_hidden: bfloat16 [16384, 1024], P(('group', 'blk')), may hold values from -6 to 6
- passage_hidden: bfloat16 [32768, 1024], P(('group', 'blk')), may hold values from -6 to 6
- w_in: bfloat16 [1024, 4096], replicated, may hold values from -0.1875 to 0.1875
- w_out: bfloat16 [4096, 1024], replicated, may hold values from -0.09375 to 0.09375
- neg_unit: int32 [16384, 64], P(('group', 'blk')), may hold values from 0 to 255, all different within a row; in each aligned block of 128 rows (0 to 127, 128 to 255, ...) at most 48 rows name the same one
- neg_row: int32 [16384, 64], P(('group', 'blk')), may hold values from 0 to 127
- rank_order: int32 [16384, 64], P(('group', 'blk')), may hold values from 0 to 63, each once within a row
Outputs:
- contrast_loss: float32 [16384], P(('group', 'blk'))
- list_loss: float32 [16384], P(('group', 'blk'))
The draws below stay inside these ranges and needn't reach their ends.
Inputs may be any that keep to these rules, and one draw needn't show every extreme that they name: `neg_unit`: each row names 64 different half-blocks; among the 128 rows of one device no half-block is named more than 48 times, and some half-block exactly 48 times. `rank_order`: each row holds every number of 0 to 63 once.
All inputs are finite; a program needn't handle non-finite values.
Results may differ from the reference program's by a relative error of at most 0.0011.
Values may be sent and summed in bfloat16 or wider, within the bound.
A program may use at most 192 MiB of HBM per device.

```python
import math
import jax
import jax.numpy as jnp
import numpy as np
from jax import lax

D = 1024
FF = 4096
NEG = 64
Q_DEV = 128
P_DEV = 256
QUERIES = 16384
PASSAGES = 32768
UNITS = 256
CAP = 48
N_BLK = 32


def draw_query_hidden(key, part):
    key = jax.random.fold_in(key, 11)
    key_base = jax.random.fold_in(key, 0)
    values = jnp.clip(jax.random.normal(key_base, (QUERIES, D), jnp.float32), -6.0, 6.0)
    return values.astype(jnp.bfloat16)


def draw_passage_hidden(key, part):
    key = jax.random.fold_in(key, 12)
    key_base = jax.random.fold_in(key, 0)
    values = jnp.clip(jax.random.normal(key_base, (PASSAGES, D), jnp.float32), -6.0, 6.0)
    return values.astype(jnp.bfloat16)


def plant(drawn, rng, smallest, top_value):
    shape = drawn.shape
    index_at = [jax.random.randint(jax.random.fold_in(rng, axis), (), 0, shape[axis]) for axis in range(len(shape))]
    drawn = drawn.at[tuple(index_at)].set(smallest)
    longest = shape.index(max(shape))
    index_at[longest] = (index_at[longest] + 1) % shape[longest]
    return drawn.at[tuple(index_at)].set(top_value)


def deal_out(key, own, number, rows, count, top, limit, slope):
    order = jax.random.permutation(key, count)
    heavy_load, usual = shares(count, rows * top, limit, slope, True), shares(count, rows * top, limit, slope, False)
    places = jnp.arange(count)

    def named(tallies, offset_by):
        used = int((tallies > 0).sum())
        fixed = max(1, used // 4)
        shifted = fixed + (places - fixed + offset_by * (used - fixed)) % max(1, count - fixed)
        return jnp.zeros((count,), jnp.int32).at[order[jnp.where(places < fixed, places, shifted)]].set(jnp.asarray(tallies, jnp.int32))

    tallies = jnp.where(number % 4 == 0, named(heavy_load, number // 4), named(usual, number - number // 4 - 1))
    mixed = jax.random.permutation(jax.random.fold_in(own, 3), count)
    giver, receiver = mixed[0:count // 2 * 2:2], mixed[1:count // 2 * 2:2]
    slack = jnp.minimum(tallies[giver] - 1, limit - tallies[receiver]) // 2
    slack = jnp.where((giver == order[0]) | (receiver == order[0]) | (tallies[receiver] == 0), 0, jnp.maximum(slack, 0))
    shifted = jax.random.randint(jax.random.fold_in(own, 4), (count // 2,), 0, 1 << 20) % (slack + 1)
    tallies = tallies.at[giver].add(-shifted).at[receiver].add(shifted)
    members = jnp.searchsorted(jnp.cumsum(tallies), jnp.arange(rows * top), side="right").astype(jnp.int32)
    grid = members.reshape(top, rows).T
    grid = grid[jax.random.permutation(jax.random.fold_in(own, 1), rows)]
    offset_by = jax.random.randint(jax.random.fold_in(own, 2), (rows, 1), 0, top)
    return jnp.take_along_axis(grid, (jnp.arange(top)[None, :] + offset_by) % top, axis=1)


def shares(number_of, total, reach, lean, full):
    weights = [(1 << 20) // math.isqrt(standing ** lean) + 1 for standing in range(1, number_of + 1)]
    largest = reach if full else min(reach, max(-(-total // number_of), total * weights[0] // sum(weights)))
    least = 1 if total - largest >= number_of - 1 else 0
    holding, rest = [largest] + [least] * (number_of - 1), total - largest - least * (number_of - 1)
    while rest > 0:
        free = [i for i in range(1, number_of) if holding[i] < largest] or [i for i in range(1, number_of) if holding[i] < reach]
        whole, left = sum([weights[i] for i in free]), rest
        for i in free:
            more = min(reach - holding[i], max(1, left * weights[i] // whole), rest)
            holding[i] = holding[i] + more
            rest = rest - more
    return np.array(holding)


def normal_values(key, shape, spread, reach, held_as=jnp.bfloat16):
    entries = jax.random.normal(key, shape, jnp.float32) * spread
    return jnp.minimum(jnp.maximum(entries, -reach), reach).astype(held_as)


def setup_inputs(seed: int = 0) -> dict:
    key_list = jax.random.split(jax.random.key(seed), 8)
    query_hidden = draw_query_hidden(jax.random.fold_in(key_list[7], 71), 0)
    passage_hidden = draw_passage_hidden(jax.random.fold_in(key_list[7], 71), 0)
    w_in = normal_values(key_list[2], (D, FF), D ** -0.5, 0.1875)
    w_out = normal_values(key_list[3], (FF, D), FF ** -0.5, 0.09375)
    neg_unit_keys = jax.random.split(jax.random.fold_in(key_list[4], 1), QUERIES // Q_DEV)
    neg_unit_turns = jax.random.permutation(jax.random.fold_in(key_list[4], 3), QUERIES // Q_DEV)
    neg_unit = jax.vmap(lambda own, number: deal_out(jax.random.fold_in(key_list[4], 2), own, number, Q_DEV, UNITS, NEG, CAP, 2))(neg_unit_keys, neg_unit_turns).reshape((QUERIES, NEG))
    neg_row = plant(jax.random.randint(key_list[5], (QUERIES, NEG), 0, P_DEV // 2), jax.random.fold_in(key_list[5], 1), 0, (P_DEV // 2) - 1).astype(jnp.int32)
    rank_order = jax.vmap(lambda own: jax.random.permutation(own, NEG))(jax.random.split(key_list[6], QUERIES)).reshape((QUERIES, NEG)).astype(jnp.int32)
    return dict(query_hidden=query_hidden, passage_hidden=passage_hidden, w_in=w_in, w_out=w_out, neg_unit=neg_unit, neg_row=neg_row, rank_order=rank_order)


def embed(hidden, w_in, w_out):
    act = jax.nn.gelu(jnp.dot(hidden, w_in, preferred_element_type=jnp.float32), approximate=True).astype(jnp.bfloat16)
    return (hidden.astype(jnp.float32) + jnp.dot(act, w_out, preferred_element_type=jnp.float32)).astype(jnp.bfloat16)


def merge_pair(first, second):
    top = jnp.maximum(first[0], second[0])
    return top, first[1] * jnp.exp(first[0] - top) + second[1] * jnp.exp(second[0] - top)


def listwise(hard, rank_order):
    ordered = jnp.take_along_axis(hard, rank_order, axis=1)
    tops, totals = lax.associative_scan(merge_pair, (ordered, jnp.ones_like(ordered)), reverse=True, axis=1)
    return jnp.mean(tops + jnp.log(totals) - ordered, axis=1)


def reference(query_hidden, passage_hidden, w_in, w_out, neg_unit, neg_row, rank_order):
    scale = 1.0 / (D ** 0.5)
    query_emb = embed(query_hidden, w_in, w_out)
    passage_emb = embed(passage_hidden, w_in, w_out)
    groups = query_emb.shape[0] // (Q_DEV * N_BLK)
    query_groups = query_emb.reshape(groups, Q_DEV * N_BLK, D)
    passage_groups = passage_emb.reshape(groups, P_DEV * N_BLK, D)

    def group_stats(pair):
        scores = jnp.dot(pair[0], pair[1].T, preferred_element_type=jnp.float32) * scale
        top = jnp.max(scores, axis=1)
        return top, jnp.sum(jnp.exp(scores - top[:, None]), axis=1)

    cycle_top, cycle_total = lax.map(group_stats, (query_groups, passage_groups))
    cycle_top = cycle_top.reshape(-1)
    cycle_total = cycle_total.reshape(-1)
    devices = query_emb.shape[0] // Q_DEV
    positives = passage_emb.reshape(devices, P_DEV, D)[:, :Q_DEV].reshape(-1, D)
    pos = jnp.sum(query_emb.astype(jnp.float32) * positives.astype(jnp.float32), axis=1) * scale
    wanted = (neg_unit // 2) * P_DEV + (neg_unit % 2) * (P_DEV // 2) + neg_row

    def hard_block(pair):
        rows = jnp.take(passage_emb, pair[1], axis=0).astype(jnp.float32)
        return jnp.einsum("qd,qkd->qk", pair[0].astype(jnp.float32), rows) * scale

    hard = lax.map(hard_block, (query_emb.reshape(devices, Q_DEV, D), wanted.reshape(devices, Q_DEV, NEG))).reshape(-1, NEG)
    top = jnp.maximum(cycle_top, jnp.max(hard, axis=1))
    total = cycle_total * jnp.exp(cycle_top - top) + jnp.sum(jnp.exp(hard - top[:, None]), axis=1)
    contrast_loss = jnp.log(total) + top - pos
    return contrast_loss, listwise(hard, rank_order)
```

```python
import math

import jax
import jax.numpy as jnp
from jax import lax
from jax.experimental import pallas as pl
from jax.experimental.pallas import tpu as pltpu
from jax.sharding import PartitionSpec as P

MESH = pl.DeviceIdType.MESH
BF16 = jnp.bfloat16
F32 = jnp.float32
I32 = jnp.int32
NEG_BIG = -1e30


def kernel(
    qh, ph, nu, nr, ro, wi_hbm, wo_hbm,
    contrast_out, list_out,
    wi, wo, x, act, qbuf, pbuf, ncode, nrow, order, code, tsend, tin, hsend, hin,
    wsem, xsem, send, recv, rqs, rqr, rts, rtr,
):
    width = x.shape[1]
    queries = 128
    passages = 256
    scale = 1.0 / math.sqrt(width)

    g = lax.axis_index("group")
    b = lax.axis_index("blk")
    core = g % 2
    zl = g // 2
    zh = b % 2
    px = (b // 2) % 4
    py = b // 8
    z = zh * 2 + zl
    r1 = px * (1 - core) + py * core
    r2 = py * (1 - core) + px * core
    me = r2 * 4 + r1

    def plane_dev(a1, a2):
        ax = a1 * (1 - core) + a2 * core
        ay = a2 * (1 - core) + a1 * core
        return (g, ay * 8 + ax * 2 + zh)

    def column_dev(az, ac):
        return ((az % 2) * 2 + ac, py * 8 + px * 2 + az // 2)

    def up(v, d):
        return (v + d) % 4

    nchunk = 4
    ff_c = wi.shape[1] // nchunk
    n_c = wo.shape[1] // nchunk

    def wi_copy(i):
        s = pl.ds(i * ff_c, ff_c)
        return pltpu.make_async_copy(wi_hbm.at[:, s], wi.at[:, s], wsem.at[i])

    def wo_copy(i):
        s = pl.ds(i * n_c, n_c)
        return pltpu.make_async_copy(wo_hbm.at[:, s], wo.at[:, s], wsem.at[nchunk + i])

    xq = pltpu.make_async_copy(qh, x.at[pl.ds(0, queries)], xsem.at[0])
    xp = pltpu.make_async_copy(ph, x.at[pl.ds(queries, passages)], xsem.at[1])
    xq.start()
    xp.start()
    for i in range(nchunk):
        wi_copy(i).start()

    barrier = pltpu.get_barrier_semaphore()

    def greet(d, _):
        pl.semaphore_signal(
            barrier, inc=1, device_id=plane_dev(up(r1, d % 4), up(r2, d // 4)), device_id_type=MESH
        )
        return 0

    lax.fori_loop(1, 16, greet, 0)
    for dev in (column_dev(z, 1 - core), column_dev(up(z, 1), core), column_dev(up(z, 3), core)):
        pl.semaphore_signal(barrier, inc=1, device_id=dev, device_id_type=MESH)

    unit = nu[...]
    vx = (unit >> 2) & 3
    vy = (unit >> 4) & 3
    v1 = vx * (1 - core) + vy * core
    v2 = vy * (1 - core) + vx * core
    within = (((unit >> 1) & 1) << 3) | (((unit >> 7) & 1) << 2) | (((unit >> 6) & 1) << 1) | (unit & 1)
    ncode[...] = (v2 << 6) | (v1 << 4) | within
    nrow[...] = nr[...]
    order[...] = ro[...]

    def build(i, _):
        ids = i * 64 + lax.broadcasted_iota(I32, (64, queries), 0)
        acc = jnp.full((64, queries), -1, I32)
        for k in range(64):
            acc = jnp.where(ids == ncode[k : k + 1, :], nrow[k : k + 1, :], acc)
        tsend[pl.ds(i * 4, 4)] = acc.reshape(4, 16, queries)
        return 0

    lax.fori_loop(0, 4, build, 0)
    acc = jnp.zeros((64, queries), I32)
    for k in range(64):
        acc = jnp.where(order[...] == k, ncode[k : k + 1, :], acc)
    code[...] = acc

    xq.wait()
    xp.wait()
    for c in range(nchunk):
        wi_copy(c).wait()
        wo_copy(c).start()

        def up_proj(j, _, c=c):
            s = pl.ds(pl.multiple_of(c * ff_c + j * 256, 256), 256)
            h = jnp.dot(x[...], wi[:, s], preferred_element_type=F32)
            act[:, s] = jax.nn.gelu(h, approximate=True).astype(BF16)
            return 0

        lax.fori_loop(0, ff_c // 256, up_proj, 0)

    pl.semaphore_wait(barrier, 18)

    def request(d):
        a1, a2 = up(r1, d % 4), up(r2, d // 4)
        return pltpu.make_async_remote_copy(
            src_ref=tsend.at[a2 * 4 + a1], dst_ref=tin.at[me],
            send_sem=rqs.at[d], recv_sem=rqr.at[d],
            device_id=plane_dev(a1, a2), device_id_type=MESH,
        )

    def request_start(d, _):
        request(d).start()
        return 0

    lax.fori_loop(1, 16, request_start, 0)
    tin[me] = tsend[me]

    own_q = pl.ds(pl.multiple_of(r1 * 128, 128), 128)
    own_p = z * 2 + core
    sent = []

    def remote(src, dst, idx, dev):
        cp = pltpu.make_async_remote_copy(
            src_ref=src, dst_ref=dst, send_sem=send.at[idx], recv_sem=recv.at[idx],
            device_id=dev, device_id_type=MESH,
        )
        return cp

    def go(src, idx, dev):
        cp = remote(src, src, idx, dev)
        cp.start()
        sent.append(cp)

    def arrived(ref, idx):
        remote(ref, ref, idx, (g, b)).wait_recv()

    for c in range(nchunk):
        wo_copy(c).wait()
        s = pl.ds(c * n_c, n_c)
        o = jnp.dot(act[0:queries, :], wo[:, s], preferred_element_type=F32)
        qbuf[r2, own_q, s] = (x[0:queries, s].astype(F32) + o).astype(BF16)

    def piece(a2, a1, lo=0, n=128):
        return qbuf.at[a2, pl.ds(pl.multiple_of(a1 * 128 + lo, 64), n)]

    r1p, r1m, r1f = up(r1, 1), up(r1, 3), up(r1, 2)
    r2p, r2m, r2f = up(r2, 1), up(r2, 3), up(r2, 2)
    dev1p, dev1m = plane_dev(r1p, r2), plane_dev(r1m, r2)
    dev2p, dev2m = plane_dev(r1, r2p), plane_dev(r1, r2m)
    cols = (r1, r1m, r1p, r1f)

    def spread(i):
        go(piece(r2, cols[i]), 4 + 2 * i, dev2p)
        go(piece(r2, cols[i]), 5 + 2 * i, dev2m)

    go(piece(r2, r1), 0, dev1p)
    go(piece(r2, r1), 1, dev1m)
    spread_own = spread
    spread_own(0)

    def down_proj(j, _):
        s = pl.ds(pl.multiple_of(j * n_c, n_c), n_c)
        o = jnp.dot(act[queries:, :], wo[:, s], preferred_element_type=F32)
        pbuf[own_p, :, s] = (x[queries:, s].astype(F32) + o).astype(BF16)
        return 0

    lax.fori_loop(0, nchunk, down_proj, 0)

    def half(az, ac, h):
        return pbuf.at[az * 2 + ac, pl.ds(h * 128, 128)]

    zp, zm, zf = up(z, 1), up(z, 3), up(z, 2)
    sib = column_dev(z, 1 - core)
    devzp, devzm = column_dev(zp, core), column_dev(zm, core)
    for h in range(2):
        go(half(z, core, h), 16 + h, sib)
        go(half(z, core, h), 18 + h, devzp)
        go(half(z, core, h), 20 + h, devzm)

    rows = lax.broadcasted_iota(I32, (128, 128), 0)
    lanes = lax.broadcasted_iota(I32, (128, 128), 1)
    dims = (((1,), (1,)), ((), ()))

    s_own = lax.dot_general(pbuf[own_p, 0:128, :], qbuf[r2, own_q, :], dims, preferred_element_type=F32)
    pos = jnp.sum(jnp.where(rows == lanes, s_own, 0.0), axis=0, keepdims=True) * scale

    def task(a2, pb, slot):
        s = lax.dot_general(pbuf[pb], qbuf[a2], dims, preferred_element_type=F32)
        for h in range(2):
            for i in range(4):
                part = s[h * 128 : (h + 1) * 128, i * 128 : (i + 1) * 128]
                want = tin[a2 * 4 + i, pl.ds(pb * 2 + h, 1), :]
                hsend[a2 * 4 + i, pl.ds(pb * 2 + h, 1), :] = jnp.sum(
                    jnp.where(rows == want, part, 0.0), axis=0, keepdims=True
                )
        if slot is not None:
            top = jnp.max(s, axis=0, keepdims=True)
            total = jnp.sum(jnp.exp((s - top) * scale), axis=0, keepdims=True)
            for i in range(4):
                w = slice(i * 128, (i + 1) * 128)
                hsend[a2 * 4 + i, 16 + 2 * slot : 17 + 2 * slot, :] = top[:, w]
                hsend[a2 * 4 + i, 17 + 2 * slot : 18 + 2 * slot, :] = total[:, w]

    def tasks(lo, hi, block, slot):
        def step(i, _):
            task(up(r2, i), block, slot)
            return 0

        lax.fori_loop(lo, hi, step, 0)

    arrived(piece(r2, r1m), 0)
    go(piece(r2, r1m, 0, 64), 2, dev1p)
    spread(1)
    arrived(piece(r2, r1p), 1)
    go(piece(r2, r1p, 64, 64), 3, dev1m)
    spread(2)
    arrived(piece(r2m, r1), 4)
    go(piece(r2m, r1), 12, dev2p)
    arrived(piece(r2p, r1), 5)
    arrived(piece(r2, r1f, 0, 64), 2)
    arrived(piece(r2, r1f, 64, 64), 3)
    spread(3)

    def request_wait(d, _):
        request(d).wait_recv()
        return 0

    lax.fori_loop(1, 16, request_wait, 0)

    tasks(0, 1, own_p, 0)
    arrived(half(z, 1 - core, 0), 16)
    arrived(half(z, 1 - core, 1), 17)
    tasks(0, 1, z * 2 + 1 - core, None)

    for h in range(2):
        arrived(half(zm, core, h), 18 + h)
        if h == 0:
            go(half(zm, core, 0), 22, devzp)
        go(half(zm, core, h), 24 + h, sib)
        arrived(half(zp, core, h), 20 + h)
        if h == 1:
            go(half(zp, core, 1), 23, devzm)
        go(half(zp, core, h), 26 + h, sib)
    arrived(piece(r2p, r1m), 7)
    go(piece(r2p, r1m), 13, dev2m)
    arrived(piece(r2p, r1p), 9)
    go(piece(r2p, r1p), 14, dev2m)
    arrived(piece(r2m, r1m), 6)
    arrived(piece(r2m, r1p), 8)
    arrived(piece(r2m, r1f), 10)
    go(piece(r2m, r1f), 15, dev2p)
    arrived(piece(r2p, r1f), 11)

    tasks(0, 1, zm * 2 + core, None)
    tasks(0, 1, zp * 2 + core, None)
    for h in range(2):
        arrived(half(zf, core, h), 22 + h)
        go(half(zf, core, h), 28 + h, sib)
    for h in range(2):
        arrived(half(zm, 1 - core, h), 24 + h)
        arrived(half(zp, 1 - core, h), 26 + h)
    for i in (1, 3):
        for blk, slot in ((own_p, 0), (z * 2 + 1 - core, None), (zm * 2 + core, None), (zp * 2 + core, None)):
            tasks(i, i + 1, blk, slot)
    tasks(0, 1, zf * 2 + core, 1)
    for i in (0, 1, 3):
        for blk in (zm * 2 + 1 - core, zp * 2 + 1 - core):
            tasks(i, i + 1, blk, None)
    for i in range(4):
        arrived(piece(r2f, cols[i]), 12 + i)
    for blk, slot in (
        (own_p, 0), (z * 2 + 1 - core, None), (zm * 2 + core, None), (zp * 2 + core, None),
        (zm * 2 + 1 - core, None), (zp * 2 + 1 - core, None),
    ):
        tasks(2, 3, blk, slot)
    tasks(1, 4, zf * 2 + core, 1)
    for h in range(2):
        arrived(half(zf, 1 - core, h), 28 + h)
    tasks(0, 4, zf * 2 + 1 - core, None)

    def answer(d):
        a1, a2 = up(r1, d % 4), up(r2, d // 4)
        return pltpu.make_async_remote_copy(
            src_ref=hsend.at[a2 * 4 + a1], dst_ref=hin.at[me],
            send_sem=rts.at[d], recv_sem=rtr.at[d],
            device_id=plane_dev(a1, a2), device_id_type=MESH,
        )

    def answer_start(d, _):
        answer(d).start()
        return 0

    def answer_wait(d, _):
        answer(d).wait_recv()
        return 0

    lax.fori_loop(1, 16, answer_start, 0)
    hin[me] = hsend[me]
    lax.fori_loop(1, 16, answer_wait, 0)

    def collect(s, ordered):
        for j in range(16):
            ordered = jnp.where(code[...] == s * 16 + j, hin[s, j : j + 1, :], ordered)
        return ordered

    ordered = lax.fori_loop(0, 16, collect, jnp.zeros((64, queries), F32)) * scale

    tops = jnp.concatenate([hin[:, 16, :], hin[:, 18, :]], axis=0) * scale
    totals = jnp.concatenate([hin[:, 17, :], hin[:, 19, :]], axis=0)
    top = jnp.maximum(jnp.max(tops, axis=0, keepdims=True), jnp.max(ordered, axis=0, keepdims=True))
    total = jnp.sum(totals * jnp.exp(tops - top), axis=0, keepdims=True)
    total = total + jnp.sum(jnp.exp(ordered - top), axis=0, keepdims=True)
    contrast_out[...] = jnp.log(total) + top - pos

    m, t = ordered, jnp.ones_like(ordered)
    for sh in (1, 2, 4, 8, 16, 32):
        m2 = jnp.concatenate([m[sh:], jnp.full((sh, queries), NEG_BIG, F32)], axis=0)
        t2 = jnp.concatenate([t[sh:], jnp.zeros((sh, queries), F32)], axis=0)
        mm = jnp.maximum(m, m2)
        t = t * jnp.exp(m - mm) + t2 * jnp.exp(m2 - mm)
        m = mm
    list_out[...] = jnp.mean(m + jnp.log(t) - ordered, axis=0, keepdims=True)

    for cp in sent:
        cp.wait_send()

    def drain(d, _):
        request(d).wait_send()
        answer(d).wait_send()
        return 0

    lax.fori_loop(1, 16, drain, 0)


def body(query_hidden, passage_hidden, w_in, w_out, neg_unit, neg_row, rank_order):
    width, ff = w_in.shape
    anyspec = pl.BlockSpec(memory_space=pl.ANY)
    vmem = pl.BlockSpec(memory_space=pltpu.VMEM)
    dma = pltpu.SemaphoreType.DMA
    contrast, listwise = pl.pallas_call(
        kernel,
        out_shape=(jax.ShapeDtypeStruct((1, 128), F32), jax.ShapeDtypeStruct((1, 128), F32)),
        in_specs=[anyspec, anyspec, vmem, vmem, vmem, anyspec, anyspec],
        out_specs=(vmem, vmem),
        scratch_shapes=[
            pltpu.VMEM((width, ff), BF16),
            pltpu.VMEM((ff, width), BF16),
            pltpu.VMEM((384, width), BF16),
            pltpu.VMEM((384, ff), BF16),
            pltpu.VMEM((4, 512, width), BF16),
            pltpu.VMEM((8, 256, width), BF16),
            pltpu.VMEM((64, 128), I32),
            pltpu.VMEM((64, 128), I32),
            pltpu.VMEM((64, 128), I32),
            pltpu.VMEM((64, 128), I32),
            pltpu.VMEM((16, 16, 128), I32),
            pltpu.VMEM((16, 16, 128), I32),
            pltpu.VMEM((16, 24, 128), F32),
            pltpu.VMEM((16, 24, 128), F32),
            dma((8,)),
            dma((2,)),
            dma((30,)),
            dma((30,)),
            dma((16,)),
            dma((16,)),
            dma((16,)),
            dma((16,)),
        ],
        compiler_params=pltpu.CompilerParams(
            collective_id=0, has_side_effects=True, vmem_limit_bytes=56 * 1024 * 1024
        ),
        name="distill",
    )(query_hidden, passage_hidden, neg_unit.T, neg_row.T, rank_order.T, w_in, w_out)
    return contrast.reshape(128), listwise.reshape(128)


def solution(mesh):
    split = P(("group", "blk"), None)
    return jax.shard_map(
        body,
        mesh=mesh,
        in_specs=(split, split, P(), P(), split, split, split),
        out_specs=(P(("group", "blk")), P(("group", "blk"))),
        check_vma=False,
    )
```

```python
import math

import jax
import jax.numpy as jnp
from jax import lax
from jax.experimental import pallas as pl
from jax.experimental.pallas import tpu as pltpu
from jax.sharding import PartitionSpec as P

MESH = pl.DeviceIdType.MESH
BF16 = jnp.bfloat16
F32 = jnp.float32
I32 = jnp.int32
NEG_BIG = -1e30


def kernel(
    qh, ph, nu, nr, ro, wi_hbm, wo_hbm,
    contrast_out, list_out,
    wi, wo, x, act, qbuf, pbuf, ncode, code, tsend, tin, hsend, hin,
    wsem, xsem, send, recv, rqs, rqr, rts, rtr,
):
    width = x.shape[1]
    queries = 128
    passages = 256
    scale = 1.0 / math.sqrt(width)

    g = lax.axis_index("group")
    b = lax.axis_index("blk")
    core = g % 2
    zl = g // 2
    zh = b % 2
    px = (b // 2) % 4
    py = b // 8
    z = zh * 2 + zl
    r1 = px * (1 - core) + py * core
    r2 = py * (1 - core) + px * core

    def plane_dev(d1, d2):
        a1, a2 = (r1 + d1) % 4, (r2 + d2) % 4
        ax = a1 * (1 - core) + a2 * core
        ay = a2 * (1 - core) + a1 * core
        return (g, ay * 8 + ax * 2 + zh)

    def column_dev(dz, dc):
        az, ac = (z + dz) % 4, (core + dc) % 2
        return ((az % 2) * 2 + ac, py * 8 + px * 2 + az // 2)

    others = [(p % 4, p // 4) for p in range(1, 16)]

    n_in, n_out = 4, 2
    c_in, c_out = wi.shape[1] // n_in, wo.shape[1] // n_out

    def wi_copy(i):
        s = pl.ds(i * c_in, c_in)
        return pltpu.make_async_copy(wi_hbm.at[:, s], wi.at[:, s], wsem.at[i])

    def wo_copy(i):
        s = pl.ds(i * c_out, c_out)
        return pltpu.make_async_copy(wo_hbm.at[:, s], wo.at[:, s], wsem.at[n_in + i])

    xq = pltpu.make_async_copy(qh, x.at[pl.ds(0, queries)], xsem.at[0])
    xp = pltpu.make_async_copy(ph, x.at[pl.ds(queries, passages)], xsem.at[1])
    xq.start()
    xp.start()
    for i in range(n_in):
        wi_copy(i).start()

    barrier = pltpu.get_barrier_semaphore()
    sib, dev_zp, dev_zm = column_dev(0, 1), column_dev(1, 0), column_dev(3, 0)
    for dev in [plane_dev(d1, d2) for d1, d2 in others] + [sib, dev_zp, dev_zm]:
        pl.semaphore_signal(barrier, inc=1, device_id=dev, device_id_type=MESH)

    unit = nu[...]
    vx = (unit >> 2) & 3
    vy = (unit >> 4) & 3
    d1 = (vx * (1 - core) + vy * core - r1) & 3
    d2 = (vy * (1 - core) + vx * core - r2) & 3
    dz = (((unit >> 1) & 1) * 2 + ((unit >> 7) & 1) - z) & 3
    dc = (((unit >> 6) & 1) - core) & 1
    hf = unit & 1
    near = 4 + hf * 4 + (dz >> 1) * 2 + dc
    within = jnp.where(dz == 0, dc * 2 + hf, jnp.where(dz == 2, 12 + dc * 2 + hf, near))
    ncode[...] = (d2 * 4 + d1) * 16 + within

    def build(i):
        ids = i * 64 + lax.broadcasted_iota(I32, (64, queries), 0)
        acc = jnp.full((64, queries), -1, I32)
        for k in range(64):
            acc = jnp.where(ids == ncode[k : k + 1, :], nr[k : k + 1, :], acc)
        tsend[i * 4 : (i + 1) * 4] = acc.reshape(4, 16, queries)

    xq.wait()
    xp.wait()
    for c in range(n_in):
        wi_copy(c).wait()
        if c < n_out:
            wo_copy(c).start()
        s = slice(c * c_in, (c + 1) * c_in)
        h = jnp.dot(x[...], wi[:, s], preferred_element_type=F32)
        act[:, s] = jax.nn.gelu(h, approximate=True).astype(BF16)
        build(c)

    pl.semaphore_wait(barrier, 18)

    def back(p):
        return (4 - p // 4) % 4 * 4 + (4 - p % 4) % 4

    def request(p):
        return pltpu.make_async_remote_copy(
            src_ref=tsend.at[p], dst_ref=tin.at[back(p)], send_sem=rqs.at[p], recv_sem=rqr.at[back(p)],
            device_id=plane_dev(p % 4, p // 4), device_id_type=MESH,
        )

    def request_in(p):
        return pltpu.make_async_remote_copy(
            src_ref=tsend.at[p], dst_ref=tin.at[p], send_sem=rqs.at[p], recv_sem=rqr.at[p],
            device_id=plane_dev(p % 4, p // 4), device_id_type=MESH,
        )

    for p in range(1, 16):
        request(p).start()
    tin[0] = tsend[0]

    names = {}
    sent = []

    def copy(src, dst, name, dev):
        i = names.setdefault(name, len(names))
        return pltpu.make_async_remote_copy(
            src_ref=src, dst_ref=dst, send_sem=send.at[i], recv_sem=recv.at[i],
            device_id=dev, device_id_type=MESH,
        )

    def go(src, dst, name, dev):
        cp = copy(src, dst, name, dev)
        cp.start()
        sent.append(cp)

    def here(dst, name):
        copy(dst, dst, name, sib).wait_recv()

    def piece(row, slot, h):
        return qbuf.at[row, pl.ds(slot * 128, 128), pl.ds(h * c_out, c_out)]

    dev1 = {1: plane_dev(1, 0), 3: plane_dev(3, 0)}
    dev2 = {1: plane_dev(0, 1), 3: plane_dev(0, 3)}

    def spread1(h):
        for d in (1, 3):
            go(piece(0, 0, h), piece(0, 4 - d, h), ("one", 4 - d, h), dev1[d])

    def spread2(slot, h):
        for d in (1, 3):
            go(piece(0, slot, h), piece(4 - d, slot, h), ("two", 4 - d, slot, h), dev2[d])

    def pass1(h):
        d = 1 if h == 0 else 3
        go(piece(0, 4 - d, h), piece(0, 2, h), ("one", 2, h), dev1[d])

    def pass2(slot, h):
        d = 1 if h == 0 else 3
        go(piece(4 - d, slot, h), piece(2, slot, h), ("two", 2, slot, h), dev2[d])

    def here1(slot, h):
        here(piece(0, slot, h), ("one", slot, h))

    def here2(row, slot, h):
        here(piece(row, slot, h), ("two", row, slot, h))

    for h in range(n_out):
        wo_copy(h).wait()
        s = slice(h * c_out, (h + 1) * c_out)
        o = jnp.dot(act[0:queries, :], wo[:, s], preferred_element_type=F32)
        qbuf[0, 0:queries, s] = (x[0:queries, s].astype(F32) + o).astype(BF16)
        spread1(h)
        spread2(0, h)

    def slot_of(dz, dc, h):
        if dz == 0:
            return dc * 2 + h
        if dz == 2:
            return 12 + dc * 2 + h
        return 4 + h * 4 + dz // 2 * 2 + dc

    def block(dz, dc, h):
        return pbuf.at[pl.ds(slot_of(dz, dc, h) * 128, 128)]

    def go_p(src, dst, dev):
        go(block(*src), block(*dst), dst, dev)

    def here_p(*dst):
        here(block(*dst), dst)

    for h in range(2):
        r = slice(queries + h * 128, queries + (h + 1) * 128)
        for c in range(n_out):
            s = slice(c * c_out, (c + 1) * c_out)
            o = jnp.dot(act[r, :], wo[:, s], preferred_element_type=F32)
            pbuf[h * 128 : (h + 1) * 128, s] = (x[r, s].astype(F32) + o).astype(BF16)
        go_p((0, 0, h), (3, 0, h), dev_zp)
        go_p((0, 0, h), (1, 0, h), dev_zm)
        go_p((0, 0, h), (0, 1, h), sib)

    acc = jnp.zeros((64, queries), I32)
    for k in range(64):
        acc = jnp.where(ro[...] == k, ncode[k : k + 1, :], acc)
    code[...] = acc
    rows = lax.broadcasted_iota(I32, (128, 128), 0)
    lanes = lax.broadcasted_iota(I32, (128, 128), 1)
    dims = (((1,), (1,)), ((), ()))
    s_own = lax.dot_general(pbuf[0:128, :], qbuf[0, 0:128, :], dims, preferred_element_type=F32)
    pos = jnp.sum(jnp.where(rows == lanes, s_own, 0.0), axis=0, keepdims=True) * scale

    def score(row, q0, q1, u0, u1):
        s = lax.dot_general(
            pbuf[u0 * 128 : u1 * 128, :], qbuf[row, q0 * 128 : q1 * 128, :], dims, preferred_element_type=F32
        )
        for q in range(q0, q1):
            w = slice((q - q0) * 128, (q - q0 + 1) * 128)
            at = row * 4 + q
            for u in range(u0, u1):
                part = s[(u - u0) * 128 : (u - u0 + 1) * 128, w]
                hit = rows == tin[at, u : u + 1, :]
                hsend[at, u : u + 1, :] = jnp.sum(jnp.where(hit, part, 0.0), axis=0, keepdims=True)
            for k, u in ((0, 0), (1, 12)):
                if u0 <= u < u1:
                    part = s[(u - u0) * 128 : (u - u0 + 2) * 128, w]
                    top = jnp.max(part, axis=0, keepdims=True)
                    hsend[at, 16 + 2 * k : 17 + 2 * k, :] = top
                    hsend[at, 17 + 2 * k : 18 + 2 * k, :] = jnp.sum(
                        jnp.exp((part - top) * scale), axis=0, keepdims=True
                    )

    def answer(p):
        return pltpu.make_async_remote_copy(
            src_ref=hsend.at[p], dst_ref=hin.at[back(p)], send_sem=rts.at[p], recv_sem=rtr.at[back(p)],
            device_id=plane_dev(p % 4, p // 4), device_id_type=MESH,
        )

    def answer_in(p):
        return pltpu.make_async_remote_copy(
            src_ref=hsend.at[p], dst_ref=hin.at[p], send_sem=rts.at[p], recv_sem=rtr.at[p],
            device_id=plane_dev(p % 4, p // 4), device_id_type=MESH,
        )

    def answer_row(row):
        for slot in range(4):
            p = row * 4 + slot
            if p == 0:
                hin[0] = hsend[0]
            else:
                answer(p).start()

    here1(3, 0)
    pass1(0)
    spread2(3, 0)
    here1(1, 0)
    spread2(1, 0)
    here2(3, 0, 0)
    pass2(0, 0)
    here1(1, 1)
    pass1(1)
    spread2(1, 1)
    here1(3, 1)
    spread2(3, 1)
    here2(1, 0, 1)
    pass2(0, 1)
    for p in range(1, 16):
        request_in(p).wait_recv()
    here_p(0, 1, 0)
    here_p(0, 1, 1)
    score(0, 0, 2, 0, 4)
    here1(2, 0)
    spread2(2, 0)
    here1(2, 1)
    spread2(2, 1)
    here_p(3, 0, 0)
    go_p((3, 0, 0), (2, 0, 0), dev_zp)
    go_p((3, 0, 0), (3, 1, 0), sib)
    here_p(1, 0, 0)
    go_p((1, 0, 0), (1, 1, 0), sib)
    score(0, 2, 4, 0, 4)
    here_p(3, 1, 0)
    here_p(1, 1, 0)
    score(0, 0, 4, 4, 8)
    here2(3, 3, 0)
    pass2(3, 0)
    here2(3, 1, 0)
    pass2(1, 0)
    here2(1, 1, 1)
    pass2(1, 1)
    here2(1, 3, 1)
    pass2(3, 1)
    here_p(1, 0, 1)
    go_p((1, 0, 1), (2, 0, 1), dev_zm)
    go_p((1, 0, 1), (1, 1, 1), sib)
    here_p(3, 0, 1)
    go_p((3, 0, 1), (3, 1, 1), sib)
    here2(1, 0, 0)
    here2(1, 1, 0)
    score(1, 0, 2, 0, 8)
    here2(3, 0, 1)
    here2(3, 1, 1)
    score(3, 0, 2, 0, 8)
    here2(3, 2, 0)
    pass2(2, 0)
    here2(1, 2, 1)
    pass2(2, 1)
    here2(1, 2, 0)
    here2(1, 3, 0)
    score(1, 2, 4, 0, 8)
    here2(3, 2, 1)
    here2(3, 3, 1)
    score(3, 2, 4, 0, 8)
    here_p(1, 1, 1)
    here_p(3, 1, 1)
    for row in (0, 1, 3):
        score(row, 0, 4, 8, 12)
    here_p(2, 0, 0)
    go_p((2, 0, 0), (2, 1, 0), sib)
    here_p(2, 0, 1)
    go_p((2, 0, 1), (2, 1, 1), sib)
    for slot in (0, 1):
        here2(2, slot, 0)
        here2(2, slot, 1)
    score(2, 0, 2, 0, 8)
    score(2, 0, 2, 8, 12)
    here_p(2, 1, 0)
    here_p(2, 1, 1)
    for row in (1, 3):
        score(row, 0, 4, 12, 16)
        answer_row(row)
    score(2, 0, 2, 12, 16)
    for slot in (2, 3):
        here2(2, slot, 0)
        here2(2, slot, 1)
    score(2, 2, 4, 0, 8)
    score(2, 2, 4, 8, 16)
    answer_row(2)
    score(0, 0, 4, 12, 16)
    answer_row(0)

    ordered = jnp.zeros((64, queries), F32)
    for p in (4, 5, 6, 7, 12, 13, 14, 15, 8, 9, 10, 11, 0, 1, 2, 3):
        if p:
            answer_in(p).wait_recv()
        for j in range(16):
            ordered = jnp.where(code[...] == p * 16 + j, hin[p, j : j + 1, :], ordered)
    ordered = ordered * scale
    tops = jnp.concatenate([hin[:, 16, :], hin[:, 18, :]], axis=0) * scale
    totals = jnp.concatenate([hin[:, 17, :], hin[:, 19, :]], axis=0)
    top = jnp.maximum(jnp.max(tops, axis=0, keepdims=True), jnp.max(ordered, axis=0, keepdims=True))
    total = jnp.sum(totals * jnp.exp(tops - top), axis=0, keepdims=True)
    total = total + jnp.sum(jnp.exp(ordered - top), axis=0, keepdims=True)
    contrast_out[...] = jnp.log(total) + top - pos

    m, t = ordered, jnp.ones_like(ordered)
    for sh in (1, 2, 4, 8, 16, 32):
        m2 = jnp.concatenate([m[sh:], jnp.full((sh, queries), NEG_BIG, F32)], axis=0)
        t2 = jnp.concatenate([t[sh:], jnp.zeros((sh, queries), F32)], axis=0)
        mm = jnp.maximum(m, m2)
        t = t * jnp.exp(m - mm) + t2 * jnp.exp(m2 - mm)
        m = mm
    list_out[...] = jnp.mean(m + jnp.log(t) - ordered, axis=0, keepdims=True)

    for cp in sent:
        cp.wait_send()
    for p in range(1, 16):
        request(p).wait_send()
        answer(p).wait_send()


def body(query_hidden, passage_hidden, w_in, w_out, neg_unit, neg_row, rank_order):
    width, ff = w_in.shape
    anyspec = pl.BlockSpec(memory_space=pl.ANY)
    vmem = pl.BlockSpec(memory_space=pltpu.VMEM)
    dma = pltpu.SemaphoreType.DMA
    contrast, listwise = pl.pallas_call(
        kernel,
        out_shape=(jax.ShapeDtypeStruct((1, 128), F32), jax.ShapeDtypeStruct((1, 128), F32)),
        in_specs=[anyspec, anyspec, vmem, vmem, vmem, anyspec, anyspec],
        out_specs=(vmem, vmem),
        scratch_shapes=[
            pltpu.VMEM((width, ff), BF16),
            pltpu.VMEM((ff, width), BF16),
            pltpu.VMEM((384, width), BF16),
            pltpu.VMEM((384, ff), BF16),
            pltpu.VMEM((4, 512, width), BF16),
            pltpu.VMEM((2048, width), BF16),
            pltpu.VMEM((64, 128), I32),
            pltpu.VMEM((64, 128), I32),
            pltpu.VMEM((16, 16, 128), I32),
            pltpu.VMEM((16, 16, 128), I32),
            pltpu.VMEM((16, 24, 128), F32),
            pltpu.VMEM((16, 24, 128), F32),
            dma((6,)),
            dma((2,)),
            dma((44,)),
            dma((44,)),
            dma((16,)),
            dma((16,)),
            dma((16,)),
            dma((16,)),
        ],
        compiler_params=pltpu.CompilerParams(
            collective_id=0, has_side_effects=True, vmem_limit_bytes=56 * 1024 * 1024
        ),
        name="distill",
    )(query_hidden, passage_hidden, neg_unit.T, neg_row.T, rank_order.T, w_in, w_out)
    return contrast.reshape(128), listwise.reshape(128)


def solution(mesh):
    split = P(("group", "blk"), None)
    return jax.shard_map(
        body,
        mesh=mesh,
        in_specs=(split, split, P(), P(), split, split, split),
        out_specs=(P(("group", "blk")), P(("group", "blk"))),
        check_vma=False,
    )
```

```python
import math

import jax
import jax.numpy as jnp
from jax import lax
from jax.experimental import pallas as pl
from jax.experimental.pallas import tpu as pltpu
from jax.sharding import PartitionSpec as P

MESH = pl.DeviceIdType.MESH
BF16 = jnp.bfloat16
F32 = jnp.float32
I32 = jnp.int32
NEG_BIG = -1e30


def kernel(
    qh, ph, nu_in, nr_in, ro_in, wi_hbm, wo_hbm,
    losses,
    wi, wo, x, act, qbuf, pbuf, nu, nr, ro, ncode, code, tsend, tin, hsend, hin,
    wsem, xsem, send, recv, rqs, rqr, rts, rtr,
):
    width = x.shape[1]
    queries = 128
    passages = 256
    scale = 1.0 / math.sqrt(width)

    g = lax.axis_index("group")
    b = lax.axis_index("blk")
    core = g % 2
    zl = g // 2
    zh = b % 2
    px = (b // 2) % 4
    py = b // 8
    z = zh * 2 + zl
    r1 = px * (1 - core) + py * core
    r2 = py * (1 - core) + px * core

    def plane_dev(d1, d2):
        a1, a2 = (r1 + d1) % 4, (r2 + d2) % 4
        ax = a1 * (1 - core) + a2 * core
        ay = a2 * (1 - core) + a1 * core
        return (g, ay * 8 + ax * 2 + zh)

    def column_dev(dz, dc):
        az, ac = (z + dz) % 4, (core + dc) % 2
        return ((az % 2) * 2 + ac, py * 8 + px * 2 + az // 2)

    others = [(p % 4, p // 4) for p in range(1, 16)]

    eighth = wi.shape[1] // 8
    cuts = [0, eighth, 2 * eighth, 4 * eighth, 6 * eighth, 8 * eighth]
    n_in, n_out = len(cuts) - 1, 2
    c_out = wo.shape[1] // n_out

    def w_copy(i):
        if i < n_in:
            s = pl.ds(cuts[i], cuts[i + 1] - cuts[i])
            return pltpu.make_async_copy(wi_hbm.at[:, s], wi.at[:, s], wsem.at[i])
        s = pl.ds((i - n_in) * c_out, c_out)
        return pltpu.make_async_copy(wo_hbm.at[:, s], wo.at[:, s], wsem.at[i])

    xq = pltpu.make_async_copy(qh, x.at[pl.ds(0, queries)], xsem.at[0])
    xp = pltpu.make_async_copy(ph, x.at[pl.ds(queries, passages)], xsem.at[1])
    xq.start()
    xp.start()
    w_copy(0).start()
    indices = [
        pltpu.make_async_copy(src, dst, xsem.at[2 + i]) for i, (src, dst) in enumerate(((nu_in, nu), (nr_in, nr), (ro_in, ro)))
    ]
    for cp in indices:
        cp.start()
    w_copy(1).start()

    barrier = pltpu.get_barrier_semaphore()
    sib, dev_zp, dev_zm = column_dev(0, 1), column_dev(1, 0), column_dev(3, 0)
    for dev in [plane_dev(d1, d2) for d1, d2 in others] + [sib, dev_zp, dev_zm]:
        pl.semaphore_signal(barrier, inc=1, device_id=dev, device_id_type=MESH)

    for cp in indices:
        cp.wait()
    unit = nu[...]
    vx = (unit >> 2) & 3
    vy = (unit >> 4) & 3
    d1 = (vx * (1 - core) + vy * core - r1) & 3
    d2 = (vy * (1 - core) + vx * core - r2) & 3
    dz = (((unit >> 1) & 1) * 2 + ((unit >> 7) & 1) - z) & 3
    dc = (((unit >> 6) & 1) - core) & 1
    hf = unit & 1
    near = 4 + (hf ^ 1 ^ (dz >> 1)) * 4 + (dz >> 1) * 2 + dc
    within = jnp.where(dz == 0, dc * 2 + hf, jnp.where(dz == 2, 12 + dc * 2 + hf, near))
    ncode[...] = (d2 * 4 + d1) * 16 + within

    def build(i):
        ids = i * 64 + lax.broadcasted_iota(I32, (64, queries), 0)
        acc = jnp.full((64, queries), -1, I32)
        for k in range(64):
            acc = jnp.where(ids == ncode[k : k + 1, :], nr[k : k + 1, :], acc)
        tsend[i * 4 : (i + 1) * 4] = acc.reshape(4, 16, queries)

    xq.wait()
    xp.wait()
    for c in range(n_in):
        if c < 2:
            build(2 * c)
        w_copy(c).wait()
        w_copy(c + 2).start()
        s = slice(cuts[c], cuts[c + 1])
        h = jnp.dot(x[...], wi[:, s], preferred_element_type=F32)
        act[:, s] = jax.nn.gelu(h, approximate=True).astype(BF16)
        if c < 2:
            build(2 * c + 1)

    def back(p):
        return (4 - p // 4) % 4 * 4 + (4 - p % 4) % 4

    def request(p):
        return pltpu.make_async_remote_copy(
            src_ref=tsend.at[p], dst_ref=tin.at[back(p)], send_sem=rqs.at[p], recv_sem=rqr.at[back(p)],
            device_id=plane_dev(p % 4, p // 4), device_id_type=MESH,
        )

    def request_in(p):
        return pltpu.make_async_remote_copy(
            src_ref=tsend.at[p], dst_ref=tin.at[p], send_sem=rqs.at[p], recv_sem=rqr.at[p],
            device_id=plane_dev(p % 4, p // 4), device_id_type=MESH,
        )

    pl.semaphore_wait(barrier, 18)
    for p in range(1, 16):
        request(p).start()
    tin[0] = tsend[0]

    names = {}
    sent = []

    def copy(src, dst, name, dev):
        i = names.setdefault(name, len(names))
        return pltpu.make_async_remote_copy(
            src_ref=src, dst_ref=dst, send_sem=send.at[i], recv_sem=recv.at[i],
            device_id=dev, device_id_type=MESH,
        )

    def go(src, dst, name, dev):
        cp = copy(src, dst, name, dev)
        cp.start()
        sent.append(cp)

    def here(dst, name):
        copy(dst, dst, name, sib).wait_recv()

    def piece(row, slot, h):
        return qbuf.at[row, pl.ds(slot * 128, 128), pl.ds(h * c_out, c_out)]

    dev1 = {1: plane_dev(1, 0), 3: plane_dev(3, 0)}
    dev2 = {1: plane_dev(0, 1), 3: plane_dev(0, 3)}

    def spread1(h):
        for d in (1, 3):
            go(piece(0, 0, h), piece(0, 4 - d, h), ("one", 4 - d, h), dev1[d])

    def spread2(slot, h):
        for d in (1, 3):
            go(piece(0, slot, h), piece(4 - d, slot, h), ("two", 4 - d, slot, h), dev2[d])

    def pass1(h):
        d = 1 if h == 0 else 3
        go(piece(0, 4 - d, h), piece(0, 2, h), ("one", 2, h), dev1[d])

    def pass2(slot, h):
        d = 1 if h == 0 else 3
        go(piece(4 - d, slot, h), piece(2, slot, h), ("two", 2, slot, h), dev2[d])

    def here1(slot, h):
        here(piece(0, slot, h), ("one", slot, h))

    def here2(row, slot, h):
        here(piece(row, slot, h), ("two", row, slot, h))

    for h in range(n_out):
        w_copy(n_in + h).wait()
        s = slice(h * c_out, (h + 1) * c_out)
        o = jnp.dot(act[0:queries, :], wo[:, s], preferred_element_type=F32)
        qbuf[0, 0:queries, s] = (x[0:queries, s].astype(F32) + o).astype(BF16)
        spread1(h)
        spread2(0, h)


    def slot_of(dz, dc, h):
        if dz == 0:
            return dc * 2 + h
        if dz == 2:
            return 12 + dc * 2 + h
        return 4 + (h ^ 1 ^ (dz // 2)) * 4 + dz // 2 * 2 + dc

    def block(dz, dc, h):
        return pbuf.at[pl.ds(slot_of(dz, dc, h) * 128, 128)]

    def go_p(src, dst, dev):
        go(block(*src), block(*dst), dst, dev)

    def here_p(*dst):
        here(block(*dst), dst)

    for c in range(n_out):
        s = slice(c * c_out, (c + 1) * c_out)
        o = jnp.dot(act[queries:, :], wo[:, s], preferred_element_type=F32)
        pbuf[0:passages, s] = (x[queries:, s].astype(F32) + o).astype(BF16)
    go_p((0, 0, 0), (3, 0, 0), dev_zp)
    go_p((0, 0, 1), (1, 0, 1), dev_zm)
    for h in range(2):
        go_p((0, 0, h), (0, 1, h), sib)

    acc = jnp.zeros((64, queries), I32)
    for k in range(64):
        acc = jnp.where(ro[...] == k, ncode[k : k + 1, :], acc)
    code[...] = acc
    rows = lax.broadcasted_iota(I32, (128, 128), 0)
    lanes = lax.broadcasted_iota(I32, (128, 128), 1)
    dims = (((1,), (1,)), ((), ()))
    s_own = lax.dot_general(pbuf[0:128, :], qbuf[0, 0:128, :], dims, preferred_element_type=F32)
    pos = jnp.sum(jnp.where(rows == lanes, s_own, 0.0), axis=0, keepdims=True) * scale

    def score(row, q0, q1, u0, u1):
        s = lax.dot_general(
            pbuf[u0 * 128 : u1 * 128, :], qbuf[row, q0 * 128 : q1 * 128, :], dims, preferred_element_type=F32
        )
        for q in range(q0, q1):
            w = slice((q - q0) * 128, (q - q0 + 1) * 128)
            at = row * 4 + q
            for u in range(u0, u1):
                part = s[(u - u0) * 128 : (u - u0 + 1) * 128, w]
                hit = rows == tin[at, u : u + 1, :]
                hsend[at, u : u + 1, :] = jnp.sum(jnp.where(hit, part, 0.0), axis=0, keepdims=True)
            for k, u in ((0, 0), (1, 12)):
                if u0 <= u < u1:
                    part = s[(u - u0) * 128 : (u - u0 + 2) * 128, w]
                    top = jnp.max(part, axis=0, keepdims=True)
                    hsend[at, 16 + 2 * k : 17 + 2 * k, :] = top
                    hsend[at, 17 + 2 * k : 18 + 2 * k, :] = jnp.sum(
                        jnp.exp((part - top) * scale), axis=0, keepdims=True
                    )

    def answer(p):
        return pltpu.make_async_remote_copy(
            src_ref=hsend.at[p], dst_ref=hin.at[back(p)], send_sem=rts.at[p], recv_sem=rtr.at[back(p)],
            device_id=plane_dev(p % 4, p // 4), device_id_type=MESH,
        )

    def answer_in(p):
        return pltpu.make_async_remote_copy(
            src_ref=hsend.at[p], dst_ref=hin.at[p], send_sem=rts.at[p], recv_sem=rtr.at[p],
            device_id=plane_dev(p % 4, p // 4), device_id_type=MESH,
        )

    def answer_row(row, slots):
        for slot in slots:
            p = row * 4 + slot
            if p == 0:
                hin[0] = hsend[0]
            else:
                answer(p).start()

    here1(3, 0)
    pass1(0)
    spread2(3, 0)
    here1(1, 0)
    spread2(1, 0)
    here2(3, 0, 0)
    pass2(0, 0)
    here1(1, 1)
    pass1(1)
    spread2(1, 1)
    here1(3, 1)
    spread2(3, 1)
    here2(1, 0, 1)
    pass2(0, 1)
    go_p((0, 0, 1), (3, 0, 1), dev_zp)
    go_p((0, 0, 0), (1, 0, 0), dev_zm)
    here_p(3, 0, 0)
    go_p((3, 0, 0), (3, 1, 0), sib)
    here_p(1, 0, 1)
    go_p((1, 0, 1), (1, 1, 1), sib)
    here1(2, 0)
    spread2(2, 0)
    here1(2, 1)
    spread2(2, 1)
    for p in range(1, 16):
        request_in(p).wait_recv()
    here_p(0, 1, 0)
    here_p(0, 1, 1)
    score(0, 0, 4, 0, 4)
    here_p(3, 1, 0)
    here_p(1, 1, 1)
    score(0, 0, 4, 4, 8)
    here2(3, 3, 0)
    pass2(3, 0)
    here2(3, 1, 0)
    pass2(1, 0)
    here2(1, 1, 1)
    pass2(1, 1)
    here2(1, 3, 1)
    pass2(3, 1)
    go_p((3, 0, 0), (2, 0, 0), dev_zp)
    go_p((1, 0, 1), (2, 0, 1), dev_zm)
    here2(1, 0, 0)
    here2(1, 1, 0)
    score(1, 0, 2, 0, 8)
    here2(3, 0, 1)
    here2(3, 1, 1)
    score(3, 0, 2, 0, 8)
    here_p(3, 0, 1)
    go_p((3, 0, 1), (3, 1, 1), sib)
    here_p(1, 0, 0)
    go_p((1, 0, 0), (1, 1, 0), sib)
    here2(3, 2, 0)
    pass2(2, 0)
    here2(1, 2, 1)
    pass2(2, 1)
    here2(1, 2, 0)
    here2(1, 3, 0)
    score(1, 2, 4, 0, 8)
    here2(3, 2, 1)
    here2(3, 3, 1)
    score(3, 2, 4, 0, 8)
    here_p(3, 1, 1)
    here_p(1, 1, 0)
    for row in (0, 1, 3):
        score(row, 0, 4, 8, 12)
    here_p(2, 0, 0)
    go_p((2, 0, 0), (2, 1, 0), sib)
    here_p(2, 0, 1)
    go_p((2, 0, 1), (2, 1, 1), sib)
    for slot in (0, 1):
        here2(2, slot, 0)
        here2(2, slot, 1)
    score(2, 0, 2, 0, 8)
    score(2, 0, 2, 8, 12)
    here_p(2, 1, 0)
    here_p(2, 1, 1)
    score(2, 0, 2, 12, 16)
    answer_row(2, (0, 1))
    for slot in (2, 3):
        here2(2, slot, 0)
        here2(2, slot, 1)
    score(2, 2, 4, 0, 8)
    score(2, 2, 4, 8, 16)
    answer_row(2, (2, 3))
    for row in (1, 3, 0):
        score(row, 0, 4, 12, 16)
        answer_row(row, (0, 1, 2, 3))

    ordered = jnp.zeros((64, queries), F32)
    for p in (8, 9, 10, 11, 4, 5, 6, 7, 12, 13, 14, 15, 0, 1, 2, 3):
        if p:
            answer_in(p).wait_recv()
        for j in range(16):
            ordered = jnp.where(code[...] == p * 16 + j, hin[p, j : j + 1, :], ordered)
    ordered = ordered * scale
    tops = jnp.concatenate([hin[:, 16, :], hin[:, 18, :]], axis=0) * scale
    totals = jnp.concatenate([hin[:, 17, :], hin[:, 19, :]], axis=0)
    top = jnp.maximum(jnp.max(tops, axis=0, keepdims=True), jnp.max(ordered, axis=0, keepdims=True))
    total = jnp.sum(totals * jnp.exp(tops - top), axis=0, keepdims=True)
    total = total + jnp.sum(jnp.exp(ordered - top), axis=0, keepdims=True)
    losses[0:1, :] = jnp.log(total) + top - pos

    m, t = ordered, jnp.ones_like(ordered)
    for sh in (1, 2, 4, 8, 16, 32):
        m2 = jnp.concatenate([m[sh:], jnp.full((sh, queries), NEG_BIG, F32)], axis=0)
        t2 = jnp.concatenate([t[sh:], jnp.zeros((sh, queries), F32)], axis=0)
        mm = jnp.maximum(m, m2)
        t = t * jnp.exp(m - mm) + t2 * jnp.exp(m2 - mm)
        m = mm
    losses[1:2, :] = jnp.mean(m + jnp.log(t) - ordered, axis=0, keepdims=True)

    for cp in sent:
        cp.wait_send()
    for p in range(1, 16):
        request(p).wait_send()
        answer(p).wait_send()


def split_rows(both, first, second):
    first[...] = both[0:1, :]
    second[...] = both[1:2, :]


def body(query_hidden, passage_hidden, w_in, w_out, neg_unit, neg_row, rank_order):
    width, ff = w_in.shape
    anyspec = pl.BlockSpec(memory_space=pl.ANY)
    vmem = pl.BlockSpec(memory_space=pltpu.VMEM)
    dma = pltpu.SemaphoreType.DMA
    losses = pl.pallas_call(
        kernel,
        out_shape=jax.ShapeDtypeStruct((8, 128), F32),
        in_specs=[anyspec] * 7,
        out_specs=vmem,
        scratch_shapes=[
            pltpu.VMEM((width, ff), BF16),
            pltpu.VMEM((ff, width), BF16),
            pltpu.VMEM((384, width), BF16),
            pltpu.VMEM((384, ff), BF16),
            pltpu.VMEM((4, 512, width), BF16),
            pltpu.VMEM((2048, width), BF16),
            pltpu.VMEM((64, 128), I32),
            pltpu.VMEM((64, 128), I32),
            pltpu.VMEM((64, 128), I32),
            pltpu.VMEM((64, 128), I32),
            pltpu.VMEM((64, 128), I32),
            pltpu.VMEM((16, 16, 128), I32),
            pltpu.VMEM((16, 16, 128), I32),
            pltpu.VMEM((16, 24, 128), F32),
            pltpu.VMEM((16, 24, 128), F32),
            dma((7,)),
            dma((5,)),
            dma((44,)),
            dma((44,)),
            dma((16,)),
            dma((16,)),
            dma((16,)),
            dma((16,)),
        ],
        compiler_params=pltpu.CompilerParams(
            collective_id=0, has_side_effects=True, vmem_limit_bytes=56 * 1024 * 1024
        ),
        name="distill",
    )(query_hidden, passage_hidden, neg_unit.T, neg_row.T, rank_order.T, w_in, w_out)
    contrast, listwise = pl.pallas_call(
        split_rows,
        out_shape=(jax.ShapeDtypeStruct((1, 128), F32), jax.ShapeDtypeStruct((1, 128), F32)),
        in_specs=[vmem],
        out_specs=(vmem, vmem),
        name="split_rows",
    )(losses)
    return contrast.reshape(128), listwise.reshape(128)


def solution(mesh):
    split = P(("group", "blk"), None)
    return jax.shard_map(
        body,
        mesh=mesh,
        in_specs=(split, split, P(), P(), split, split, split),
        out_specs=(P(("group", "blk")), P(("group", "blk"))),
        check_vma=False,
    )
```

```python
import math

import jax
import jax.numpy as jnp
from jax import lax
from jax.experimental import pallas as pl
from jax.experimental.pallas import tpu as pltpu
from jax.sharding import PartitionSpec as P

MESH = pl.DeviceIdType.MESH
BF16 = jnp.bfloat16
F32 = jnp.float32
I32 = jnp.int32
NEG_BIG = -1e30


def kernel(
    qh, ph, nu_in, nr_in, ro_in, wi_hbm, wo_hbm,
    losses,
    wi, wo, x, act, qbuf, pbuf, nu, nr, ro, ncode, code, tsend, tin, hsend, hin,
    wsem, xsem, send, recv, rqs, rqr, rts, rtr,
):
    width = x.shape[1]
    queries = 128
    passages = 256
    scale = 1.0 / math.sqrt(width)

    g = lax.axis_index("group")
    b = lax.axis_index("blk")
    core = g % 2
    zl = g // 2
    zh = b % 2
    px = (b // 2) % 4
    py = b // 8
    z = zh * 2 + zl
    r1 = px * (1 - core) + py * core
    r2 = py * (1 - core) + px * core

    def plane_dev(d1, d2):
        a1, a2 = (r1 + d1) % 4, (r2 + d2) % 4
        ax = a1 * (1 - core) + a2 * core
        ay = a2 * (1 - core) + a1 * core
        return (g, ay * 8 + ax * 2 + zh)

    def column_dev(dz, dc):
        az, ac = (z + dz) % 4, (core + dc) % 2
        return ((az % 2) * 2 + ac, py * 8 + px * 2 + az // 2)

    others = [(p % 4, p // 4) for p in range(1, 16)]

    eighth = wi.shape[1] // 8
    cuts = [0, eighth, 2 * eighth, 4 * eighth, 6 * eighth, 8 * eighth]
    n_in, n_out = len(cuts) - 1, 2
    c_out = wo.shape[1] // n_out

    def w_copy(i):
        if i < n_in:
            s = pl.ds(cuts[i], cuts[i + 1] - cuts[i])
            return pltpu.make_async_copy(wi_hbm.at[:, s], wi.at[:, s], wsem.at[i])
        s = pl.ds((i - n_in) * c_out, c_out)
        return pltpu.make_async_copy(wo_hbm.at[:, s], wo.at[:, s], wsem.at[i])

    xq = pltpu.make_async_copy(qh, x.at[pl.ds(0, queries)], xsem.at[0])
    xp = pltpu.make_async_copy(ph, x.at[pl.ds(queries, passages)], xsem.at[1])
    xq.start()
    xp.start()
    w_copy(0).start()
    indices = [
        pltpu.make_async_copy(src, dst, xsem.at[2 + i]) for i, (src, dst) in enumerate(((nu_in, nu), (nr_in, nr), (ro_in, ro)))
    ]
    for cp in indices:
        cp.start()
    w_copy(1).start()

    barrier = pltpu.get_barrier_semaphore()
    sib, dev_zp, dev_zm = column_dev(0, 1), column_dev(1, 0), column_dev(3, 0)
    for dev in [plane_dev(d1, d2) for d1, d2 in others] + [sib, dev_zp, dev_zm]:
        pl.semaphore_signal(barrier, inc=1, device_id=dev, device_id_type=MESH)

    for cp in indices:
        cp.wait()
    unit = nu[...]
    vx = (unit >> 2) & 3
    vy = (unit >> 4) & 3
    d1 = (vx * (1 - core) + vy * core - r1) & 3
    d2 = (vy * (1 - core) + vx * core - r2) & 3
    dz = (((unit >> 1) & 1) * 2 + ((unit >> 7) & 1) - z) & 3
    dc = (((unit >> 6) & 1) - core) & 1
    hf = unit & 1
    near = 4 + (hf ^ 1 ^ (dz >> 1)) * 4 + (dz >> 1) * 2 + dc
    within = jnp.where(dz == 0, dc * 2 + hf, jnp.where(dz == 2, 12 + dc * 2 + hf, near))
    ncode[...] = (d2 * 4 + d1) * 16 + within

    def build(i):
        ids = i * 64 + lax.broadcasted_iota(I32, (64, queries), 0)
        acc = jnp.full((64, queries), -1, I32)
        for k in range(64):
            acc = jnp.where(ids == ncode[k : k + 1, :], nr[k : k + 1, :], acc)
        tsend[i * 4 : (i + 1) * 4] = acc.reshape(4, 16, queries)

    xq.wait()
    xp.wait()
    for c in range(n_in):
        if c < 2:
            build(2 * c)
        w_copy(c).wait()
        w_copy(c + 2).start()
        s = slice(cuts[c], cuts[c + 1])
        h = jnp.dot(x[...], wi[:, s], preferred_element_type=F32)
        act[:, s] = jax.nn.gelu(h, approximate=True).astype(BF16)
        if c < 2:
            build(2 * c + 1)

    def back(p):
        return (4 - p // 4) % 4 * 4 + (4 - p % 4) % 4

    def request(p):
        return pltpu.make_async_remote_copy(
            src_ref=tsend.at[p], dst_ref=tin.at[back(p)], send_sem=rqs.at[p], recv_sem=rqr.at[back(p)],
            device_id=plane_dev(p % 4, p // 4), device_id_type=MESH,
        )

    def request_in(p):
        return pltpu.make_async_remote_copy(
            src_ref=tsend.at[p], dst_ref=tin.at[p], send_sem=rqs.at[p], recv_sem=rqr.at[p],
            device_id=plane_dev(p % 4, p // 4), device_id_type=MESH,
        )

    pl.semaphore_wait(barrier, 18)
    for p in range(1, 16):
        request(p).start()
    tin[0] = tsend[0]

    names = {}
    sent = []

    def copy(src, dst, name, dev):
        i = names.setdefault(name, len(names))
        return pltpu.make_async_remote_copy(
            src_ref=src, dst_ref=dst, send_sem=send.at[i], recv_sem=recv.at[i],
            device_id=dev, device_id_type=MESH,
        )

    def go(src, dst, name, dev):
        cp = copy(src, dst, name, dev)
        cp.start()
        sent.append(cp)

    def here(dst, name):
        copy(dst, dst, name, sib).wait_recv()

    def piece(row, slot, h):
        return qbuf.at[row, pl.ds(slot * 128, 128), pl.ds(h * c_out, c_out)]

    dev1 = {1: plane_dev(1, 0), 3: plane_dev(3, 0)}
    dev2 = {1: plane_dev(0, 1), 3: plane_dev(0, 3)}

    def spread1(h):
        for d in (1, 3):
            go(piece(0, 0, h), piece(0, 4 - d, h), ("one", 4 - d, h), dev1[d])

    def spread2(slot, h):
        for d in (1, 3):
            go(piece(0, slot, h), piece(4 - d, slot, h), ("two", 4 - d, slot, h), dev2[d])

    def pass1(h):
        d = 1 if h == 0 else 3
        go(piece(0, 4 - d, h), piece(0, 2, h), ("one", 2, h), dev1[d])

    def pass2(slot, h):
        d = 1 if h == 0 else 3
        go(piece(4 - d, slot, h), piece(2, slot, h), ("two", 2, slot, h), dev2[d])

    def here1(slot, h):
        here(piece(0, slot, h), ("one", slot, h))

    def here2(row, slot, h):
        here(piece(row, slot, h), ("two", row, slot, h))

    for h in range(n_out):
        w_copy(n_in + h).wait()
        s = slice(h * c_out, (h + 1) * c_out)
        o = jnp.dot(act[0:queries, :], wo[:, s], preferred_element_type=F32)
        qbuf[0, 0:queries, s] = (x[0:queries, s].astype(F32) + o).astype(BF16)
        spread1(h)
        spread2(0, h)


    def slot_of(dz, dc, h):
        if dz == 0:
            return dc * 2 + h
        if dz == 2:
            return 12 + dc * 2 + h
        return 4 + (h ^ 1 ^ (dz // 2)) * 4 + dz // 2 * 2 + dc

    def block(dz, dc, h):
        return pbuf.at[pl.ds(slot_of(dz, dc, h) * 128, 128)]

    def go_p(src, dst, dev):
        go(block(*src), block(*dst), dst, dev)

    def here_p(*dst):
        here(block(*dst), dst)

    for c in range(n_out):
        s = slice(c * c_out, (c + 1) * c_out)
        o = jnp.dot(act[queries:, :], wo[:, s], preferred_element_type=F32)
        pbuf[0:passages, s] = (x[queries:, s].astype(F32) + o).astype(BF16)
    go_p((0, 0, 0), (3, 0, 0), dev_zp)
    go_p((0, 0, 1), (1, 0, 1), dev_zm)
    for h in range(2):
        go_p((0, 0, h), (0, 1, h), sib)

    acc = jnp.zeros((64, queries), I32)
    for k in range(64):
        acc = jnp.where(ro[...] == k, ncode[k : k + 1, :], acc)
    code[...] = acc
    rows = lax.broadcasted_iota(I32, (128, 128), 0)
    lanes = lax.broadcasted_iota(I32, (128, 128), 1)
    dims = (((1,), (1,)), ((), ()))
    s_own = lax.dot_general(pbuf[0:128, :], qbuf[0, 0:128, :], dims, preferred_element_type=F32)
    pos = jnp.sum(jnp.where(rows == lanes, s_own, 0.0), axis=0, keepdims=True) * scale

    def score(row, q0, q1, u0, u1):
        s = lax.dot_general(
            pbuf[u0 * 128 : u1 * 128, :], qbuf[row, q0 * 128 : q1 * 128, :], dims, preferred_element_type=F32
        )
        for q in range(q0, q1):
            w = slice((q - q0) * 128, (q - q0 + 1) * 128)
            at = row * 4 + q
            for u in range(u0, u1):
                part = s[(u - u0) * 128 : (u - u0 + 1) * 128, w]
                hit = rows == tin[at, u : u + 1, :]
                hsend[at, u : u + 1, :] = jnp.sum(jnp.where(hit, part, 0.0), axis=0, keepdims=True)
            for k, u in ((0, 0), (1, 12)):
                if u0 <= u < u1:
                    part = s[(u - u0) * 128 : (u - u0 + 2) * 128, w]
                    top = jnp.max(part, axis=0, keepdims=True)
                    hsend[at, 16 + 2 * k : 17 + 2 * k, :] = top
                    hsend[at, 17 + 2 * k : 18 + 2 * k, :] = jnp.sum(
                        jnp.exp((part - top) * scale), axis=0, keepdims=True
                    )

    def answer(p):
        return pltpu.make_async_remote_copy(
            src_ref=hsend.at[p], dst_ref=hin.at[back(p)], send_sem=rts.at[p], recv_sem=rtr.at[back(p)],
            device_id=plane_dev(p % 4, p // 4), device_id_type=MESH,
        )

    def answer_in(p):
        return pltpu.make_async_remote_copy(
            src_ref=hsend.at[p], dst_ref=hin.at[p], send_sem=rts.at[p], recv_sem=rtr.at[p],
            device_id=plane_dev(p % 4, p // 4), device_id_type=MESH,
        )

    def answer_row(row, slots):
        for slot in slots:
            p = row * 4 + slot
            if p == 0:
                hin[0] = hsend[0]
            else:
                answer(p).start()

    here1(3, 0)
    pass1(0)
    spread2(3, 0)
    here1(1, 0)
    spread2(1, 0)
    here2(3, 0, 0)
    pass2(0, 0)
    here1(1, 1)
    pass1(1)
    spread2(1, 1)
    here1(3, 1)
    spread2(3, 1)
    here2(1, 0, 1)
    pass2(0, 1)
    go_p((0, 0, 1), (3, 0, 1), dev_zp)
    go_p((0, 0, 0), (1, 0, 0), dev_zm)
    here_p(3, 0, 0)
    go_p((3, 0, 0), (2, 0, 0), dev_zp)
    go_p((3, 0, 0), (3, 1, 0), sib)
    here_p(1, 0, 1)
    go_p((1, 0, 1), (2, 0, 1), dev_zm)
    go_p((1, 0, 1), (1, 1, 1), sib)
    here1(2, 0)
    spread2(2, 0)
    here1(2, 1)
    spread2(2, 1)
    for p in range(1, 16):
        request_in(p).wait_recv()
    here_p(0, 1, 0)
    here_p(0, 1, 1)
    score(0, 0, 4, 0, 4)
    here_p(3, 1, 0)
    here_p(1, 1, 1)
    score(0, 0, 4, 4, 8)
    here2(3, 3, 0)
    pass2(3, 0)
    here2(3, 1, 0)
    pass2(1, 0)
    here2(1, 1, 1)
    pass2(1, 1)
    here2(1, 3, 1)
    pass2(3, 1)
    here2(1, 0, 0)
    here2(1, 1, 0)
    score(1, 0, 2, 0, 8)
    here2(3, 0, 1)
    here2(3, 1, 1)
    score(3, 0, 2, 0, 8)
    here_p(3, 0, 1)
    go_p((3, 0, 1), (3, 1, 1), sib)
    here_p(1, 0, 0)
    go_p((1, 0, 0), (1, 1, 0), sib)
    here2(3, 2, 0)
    pass2(2, 0)
    here2(1, 2, 1)
    pass2(2, 1)
    here2(1, 2, 0)
    here2(1, 3, 0)
    score(1, 2, 4, 0, 8)
    here2(3, 2, 1)
    here2(3, 3, 1)
    score(3, 2, 4, 0, 8)
    here_p(3, 1, 1)
    here_p(1, 1, 0)
    score(1, 0, 4, 8, 12)
    here_p(2, 0, 0)
    go_p((2, 0, 0), (2, 1, 0), sib)
    here_p(2, 0, 1)
    go_p((2, 0, 1), (2, 1, 1), sib)
    for row in (0, 3):
        score(row, 0, 4, 8, 12)
    for slot in (0, 1):
        here2(2, slot, 0)
        here2(2, slot, 1)
    score(2, 0, 2, 0, 8)
    score(2, 0, 2, 8, 12)
    here_p(2, 1, 0)
    here_p(2, 1, 1)
    score(2, 0, 2, 12, 16)
    answer_row(2, (0, 1))
    for slot in (2, 3):
        here2(2, slot, 0)
        here2(2, slot, 1)
    score(2, 2, 4, 0, 8)
    score(2, 2, 4, 8, 16)
    answer_row(2, (2, 3))
    for row in (1, 3, 0):
        score(row, 0, 4, 12, 16)
        answer_row(row, (0, 1, 2, 3))

    ordered = jnp.zeros((64, queries), F32)
    for p in (8, 9, 10, 11, 4, 5, 6, 7, 12, 13, 14, 15, 0, 1, 2, 3):
        if p:
            answer_in(p).wait_recv()
        for j in range(16):
            ordered = jnp.where(code[...] == p * 16 + j, hin[p, j : j + 1, :], ordered)
    ordered = ordered * scale
    tops = jnp.concatenate([hin[:, 16, :], hin[:, 18, :]], axis=0) * scale
    totals = jnp.concatenate([hin[:, 17, :], hin[:, 19, :]], axis=0)
    top = jnp.maximum(jnp.max(tops, axis=0, keepdims=True), jnp.max(ordered, axis=0, keepdims=True))
    total = jnp.sum(totals * jnp.exp(tops - top), axis=0, keepdims=True)
    total = total + jnp.sum(jnp.exp(ordered - top), axis=0, keepdims=True)
    losses[0:1, :] = jnp.log(total) + top - pos

    m, t = ordered, jnp.ones_like(ordered)
    for sh in (1, 2, 4, 8, 16, 32):
        m2 = jnp.concatenate([m[sh:], jnp.full((sh, queries), NEG_BIG, F32)], axis=0)
        t2 = jnp.concatenate([t[sh:], jnp.zeros((sh, queries), F32)], axis=0)
        mm = jnp.maximum(m, m2)
        t = t * jnp.exp(m - mm) + t2 * jnp.exp(m2 - mm)
        m = mm
    losses[1:2, :] = jnp.mean(m + jnp.log(t) - ordered, axis=0, keepdims=True)

    for cp in sent:
        cp.wait_send()
    for p in range(1, 16):
        request(p).wait_send()
        answer(p).wait_send()


def split_rows(both, first, second):
    first[...] = both[0:1, :]
    second[...] = both[1:2, :]


def body(query_hidden, passage_hidden, w_in, w_out, neg_unit, neg_row, rank_order):
    width, ff = w_in.shape
    anyspec = pl.BlockSpec(memory_space=pl.ANY)
    vmem = pl.BlockSpec(memory_space=pltpu.VMEM)
    dma = pltpu.SemaphoreType.DMA
    losses = pl.pallas_call(
        kernel,
        out_shape=jax.ShapeDtypeStruct((8, 128), F32),
        in_specs=[anyspec] * 7,
        out_specs=vmem,
        scratch_shapes=[
            pltpu.VMEM((width, ff), BF16),
            pltpu.VMEM((ff, width), BF16),
            pltpu.VMEM((384, width), BF16),
            pltpu.VMEM((384, ff), BF16),
            pltpu.VMEM((4, 512, width), BF16),
            pltpu.VMEM((2048, width), BF16),
            pltpu.VMEM((64, 128), I32),
            pltpu.VMEM((64, 128), I32),
            pltpu.VMEM((64, 128), I32),
            pltpu.VMEM((64, 128), I32),
            pltpu.VMEM((64, 128), I32),
            pltpu.VMEM((16, 16, 128), I32),
            pltpu.VMEM((16, 16, 128), I32),
            pltpu.VMEM((16, 24, 128), F32),
            pltpu.VMEM((16, 24, 128), F32),
            dma((7,)),
            dma((5,)),
            dma((44,)),
            dma((44,)),
            dma((16,)),
            dma((16,)),
            dma((16,)),
            dma((16,)),
        ],
        compiler_params=pltpu.CompilerParams(
            collective_id=0, has_side_effects=True, vmem_limit_bytes=56 * 1024 * 1024
        ),
        name="distill",
    )(query_hidden, passage_hidden, neg_unit.T, neg_row.T, rank_order.T, w_in, w_out)
    contrast, listwise = pl.pallas_call(
        split_rows,
        out_shape=(jax.ShapeDtypeStruct((1, 128), F32), jax.ShapeDtypeStruct((1, 128), F32)),
        in_specs=[vmem],
        out_specs=(vmem, vmem),
        name="split_rows",
    )(losses)
    return contrast.reshape(128), listwise.reshape(128)


def solution(mesh):
    split = P(("group", "blk"), None)
    return jax.shard_map(
        body,
        mesh=mesh,
        in_specs=(split, split, P(), P(), split, split, split),
        out_specs=(P(("group", "blk")), P(("group", "blk"))),
        check_vma=False,
    )
```
